32 devices in a mesh: groups: 2 (over x), facet: 16 (over z, y, core).
Axes of the slice: x: 2, y: 2, z: 4, core: 2. Of those that a mesh axis runs over, the one named last changes fastest.
Arguments:
- sky_strips: bfloat16 [2, 16, 16384], P(None, 'groups', 'facet'), parts along dimension 1, may hold values from -6 to 6
- prolate: float32 [1024], replicated, may hold values from 0.25 to 1
- subgrid_offset: int32 [16], replicated, may hold values from 0 to 16383
- owner: int32 [16], replicated, may hold values from 0 to 15, as said below
- observed: float32 [64, 2, 8, 8192], P(('groups', 'facet')), parts along dimension 0, may hold values from -6 to 6
- vis_uv: float32 [64, 8192], P(('groups', 'facet')), parts along dimension 0, may hold values from 0 to 512
- vis_count: int32 [64], P(('groups', 'facet')), parts along dimension 0, may hold values from 1 to 8192
Outputs:
- residual_vis: bfloat16 [64, 2, 8, 8192], P(('groups', 'facet')), parts along dimension 0
- image_update: float32 [2, 16, 16384], P(None, 'groups', 'facet'), parts along dimension 1
The draws below stay inside these ranges and needn't reach their ends.
There are 2 independent parts, one for each index of `groups`. The reference program is written for one: setup_inputs(seed, part) draws one part's arguments, and reference() takes and returns one part's arrays. A program takes and returns all parts, laid end to end along the dimension named above; an argument that names none is the same for every part. Nothing has to cross between parts.
Inputs may be any that keep to these rules, and one draw needn't show every extreme that they name: `owner`: each index of facet owns at most 2 subgrids, and some index owns exactly 2.
All inputs are finite; a program needn't handle non-finite values.
Results may differ from the reference program's by a relative error of at most 0.01.
Values may be sent and summed in bfloat16 or wider, within the bound.
A program may use at most 64 MiB of HBM per device.

```python
import math
import jax
import jax.numpy as jnp
from jax import lax

FACET_WIDTH = 1024
POINTS = 512
ROWS = 8
VIS = 8192
SLOTS = 2
SUBGRIDS = 16
SLOT_TOTAL = 32
GRID = 16384
N_FACET = 16


def draw_owner(key, part):
    stream = jax.random.fold_in(key, 11)
    first_key, second_key, third_key = jax.random.split(stream, 3)
    others = jax.random.permutation(first_key, SLOT_TOTAL - 2)[:SUBGRIDS - 2] + 2
    chosen = jnp.concatenate([jnp.array([0, 1], dtype=jnp.int32), others.astype(jnp.int32)])
    chosen = chosen[jax.random.permutation(second_key, SUBGRIDS)]
    relabel = jax.random.permutation(third_key, N_FACET).astype(jnp.int32)
    return relabel[chosen // SLOTS]


def with_ends(result, stream_key, smallest, largest):
    place = [jax.random.randint(jax.random.fold_in(stream_key, axis), (), 0, length) for axis, length in enumerate(result.shape)]
    widest = result.shape.index(max(result.shape))
    next_to = place[:widest] + [(place[widest] + 1) % result.shape[widest]] + place[widest + 1:]
    return result.at[tuple(place)].set(smallest).at[tuple(next_to)].set(largest)


def block_levels(own_key, extent, cuts, low, largest):
    factor_of, own = 1.0, jax.random.fold_in(own_key, 6)
    for dim, parts in cuts:
        heights = jnp.exp(jax.random.uniform(jax.random.fold_in(own, dim), (parts,), jnp.float32, low / len(cuts), largest / len(cuts)))
        factor_of = factor_of * jnp.repeat(heights, extent[dim] // parts).reshape([-1 if axis == dim else 1 for axis in range(len(extent))])
    return factor_of


def gaussian(rng, extent, scale, limit, shards=(), kind=jnp.bfloat16):
    values = scale * jax.random.normal(rng, extent, jnp.float32)
    if shards:
        values = values * block_levels(rng, extent, shards, -0.22, 0.18)
    return jnp.clip(values, -limit, limit).astype(kind)


def setup_inputs(seed: int = 0, part: int = 0) -> dict:
    streams_of = jax.random.split(jax.random.key(seed), 8)
    part_splits = jax.random.split(jax.random.fold_in(streams_of[7], part), 8)
    return {
        "sky_strips": gaussian(part_splits[0], (2, ROWS, GRID), 1.0, 6.0, ((2, 16),)),
        "prolate": jnp.clip(jnp.exp(jax.random.uniform(streams_of[1], (FACET_WIDTH,), jnp.float32, math.log(0.25), math.log(1.0))), 0.25, 1.0),
        "subgrid_offset": with_ends(jax.random.randint(streams_of[2], (SUBGRIDS,), 0, GRID), jax.random.fold_in(streams_of[2], 1), 0, GRID - 1).astype(jnp.int32),
        "owner": draw_owner(jax.random.fold_in(streams_of[7], 71), part),
        "observed": gaussian(part_splits[4], (SLOT_TOTAL, 2, ROWS, VIS), 1.0, 6.0, ((0, 16),), jnp.float32),
        "vis_uv": jnp.clip(512.0 * jax.random.uniform(part_splits[5], (SLOT_TOTAL, VIS), jnp.float32) ** block_levels(part_splits[5], (SLOT_TOTAL, VIS), ((0, 16),), -0.2, 0.2), 0.0, 512.0),
        "vis_count": with_ends(jax.random.randint(part_splits[6], (SLOT_TOTAL,), 1, VIS + 1), jax.random.fold_in(part_splits[6], 1), 1, VIS).astype(jnp.int32),
    }


TWO_PI = 6.283185307179586

def matmul(first, second):
    return jnp.dot(first.astype(jnp.float32), second.astype(jnp.float32), precision=lax.Precision.HIGHEST)

def modular_product(factor, second, modulus):
    upper = second // 256
    lower = second % 256
    return (factor * lower % modulus + factor * upper % modulus * 256 % modulus) % modulus

def phasor(index, modulus):
    angle = index.astype(jnp.float32) * (TWO_PI / modulus)
    return (jnp.cos(angle), jnp.sin(angle))

def forward_table(columns, points, modulus):
    across = jnp.arange(columns, dtype=jnp.int32)[:, None]
    along = jnp.arange(points, dtype=jnp.int32)[None, :]
    cosine, sine = phasor(modular_product(across, along, modulus), modulus)
    upper_half = jnp.concatenate([cosine, -sine], 1)
    lower_half = jnp.concatenate([sine, cosine], 1)
    return jnp.concatenate([upper_half, lower_half], 0).astype(jnp.bfloat16)

def facet_terms(strip_re, strip_im, weight, columns, anchor, offsets, phase_table, modulus, points, product):
    scaled_re = strip_re * weight
    scaled_im = strip_im * weight
    cosine, sine = phasor(modular_product(columns[None, :], offsets[:, None], modulus), modulus)
    mod_re = scaled_re[None] * cosine[:, None] + scaled_im[None] * sine[:, None]
    mod_im = scaled_im[None] * cosine[:, None] - scaled_re[None] * sine[:, None]
    subgrid_count = offsets.shape[0]
    strip_rows = strip_re.shape[0]
    modulated = jnp.concatenate([mod_re, mod_im], -1).astype(jnp.bfloat16).reshape(subgrid_count * strip_rows, -1)
    raw = product(modulated, phase_table).reshape(subgrid_count, strip_rows, 2 * points)
    along = jnp.arange(points, dtype=jnp.int32)
    shifted = (along[None, :] + offsets[:, None]) % modulus
    out_cos, out_sin = phasor(modular_product(anchor, shifted, modulus), modulus)
    raw_re = raw[..., :points]
    raw_im = raw[..., points:]
    factor_scale = 1.0 / math.sqrt(modulus)
    term_re = (raw_re * out_cos[:, None] + raw_im * out_sin[:, None]) * factor_scale
    term_im = (raw_im * out_cos[:, None] - raw_re * out_sin[:, None]) * factor_scale
    return jnp.concatenate([term_re, term_im], -1)

def slot_layout(owner, slots, total):
    subgrid_count = owner.shape[0]
    index = jnp.arange(subgrid_count, dtype=jnp.int32)
    same = owner[:, None] == owner[None, :]
    before = index[None, :] < index[:, None]
    ranked = lax.optimization_barrier(jnp.sum(same & before, axis=1)).astype(jnp.int32)
    slot_of = owner.astype(jnp.int32) * slots + ranked
    wanted = jnp.arange(total, dtype=jnp.int32)
    matches = slot_of[None, :] == wanted[:, None]
    is_held = jnp.any(matches, axis=1)
    slot_ids = lax.optimization_barrier(jnp.sum(jnp.where(matches, index[None, :], 0), axis=1)).astype(jnp.int32)
    return (slot_ids, is_held)

def degrid_slot(grid, observed_slot, coords, live_count, is_held, block, points, product):
    strip_rows = grid.shape[0]
    total = coords.shape[0]
    blocks = total // block
    obs_blocks = observed_slot.reshape(2, strip_rows, blocks, block).transpose(2, 0, 1, 3)
    coord_blocks = coords.reshape(blocks, block)
    along = jnp.arange(points, dtype=jnp.int32).astype(jnp.float32)
    within = jnp.arange(block, dtype=jnp.int32)

    def visit(carry, inputs):
        position, coord_block, obs_block = inputs
        turns = along[:, None] * coord_block[None, :] / points
        fraction = turns - jnp.floor(turns)
        cosine = jnp.cos(TWO_PI * fraction)
        sine = jnp.sin(TWO_PI * fraction)
        degrid_table = jnp.concatenate([jnp.concatenate([cosine, sine], 1), jnp.concatenate([-sine, cosine], 1)], 0).astype(jnp.bfloat16)
        model = product(grid, degrid_table) / math.sqrt(points)
        live = (position * block + within < live_count) & is_held
        resid_re = jnp.where(live[None, :], obs_block[0] - model[:, :block], jnp.float32(0.0))
        resid_im = jnp.where(live[None, :], obs_block[1] - model[:, block:], jnp.float32(0.0))
        residual = jnp.concatenate([resid_re, resid_im], -1).astype(jnp.bfloat16)
        carry = carry + product(residual, degrid_table.T)
        return (carry, residual)
    initial = jnp.zeros((strip_rows, 2 * points), jnp.float32)
    total_sum, residuals = lax.scan(visit, initial, (jnp.arange(blocks, dtype=jnp.int32), coord_blocks, obs_blocks))
    update = (total_sum / math.sqrt(total)).astype(jnp.bfloat16)
    resid_re = residuals[..., :block].transpose(1, 0, 2).reshape(strip_rows, total)
    resid_im = residuals[..., block:].transpose(1, 0, 2).reshape(strip_rows, total)
    return (update, jnp.stack([resid_re, resid_im], 0))

def lift_back(updates, slot_ids, offsets, anchor, phase_table, modulus, points, product):
    number = updates.shape[0]
    strip_rows = updates.shape[1]
    subgrid_count = offsets.shape[0]
    chosen = lax.optimization_barrier(jnp.sum(jnp.where(slot_ids[:, None] == jnp.arange(subgrid_count, dtype=jnp.int32)[None, :], offsets[None, :], 0), axis=1)).astype(jnp.int32)
    along = jnp.arange(points, dtype=jnp.int32)
    cosine, sine = phasor(modular_product(anchor, (along[None, :] + chosen[:, None]) % modulus, modulus), modulus)
    upd_re = updates[..., :points].astype(jnp.float32)
    upd_im = updates[..., points:].astype(jnp.float32)
    lift_re = upd_re * cosine[:, None] - upd_im * sine[:, None]
    lift_im = upd_re * sine[:, None] + upd_im * cosine[:, None]
    lifted = jnp.concatenate([lift_re, lift_im], -1).astype(jnp.bfloat16).reshape(number * strip_rows, 2 * points)
    width = phase_table.shape[0] // 2
    back = product(lifted, phase_table.T).reshape(number, strip_rows, 2 * width)
    across = jnp.arange(width, dtype=jnp.int32)
    col_cos, col_sin = phasor(modular_product(across[None, :], chosen[:, None], modulus), modulus)
    back_re = back[..., :width]
    back_im = back[..., width:]
    out_re = lax.optimization_barrier(jnp.sum(back_re * col_cos[:, None] - back_im * col_sin[:, None], axis=0))
    out_im = lax.optimization_barrier(jnp.sum(back_re * col_sin[:, None] + back_im * col_cos[:, None], axis=0))
    return jnp.concatenate([out_re, out_im], -1)

def reference(sky_strips, prolate, subgrid_offset, owner, observed, vis_uv, vis_count):
    modulus = FACET_WIDTH * N_FACET
    phase_table = forward_table(FACET_WIDTH, POINTS, modulus)
    columns = jnp.arange(FACET_WIDTH, dtype=jnp.int32)
    offsets = subgrid_offset.astype(jnp.int32)

    def accumulate(total, facet):
        anchor = facet * FACET_WIDTH
        strip = lax.dynamic_slice_in_dim(sky_strips, anchor, FACET_WIDTH, 2).astype(jnp.float32)
        terms = facet_terms(strip[0], strip[1], prolate, columns, anchor, offsets, phase_table, modulus, POINTS, matmul)
        return (total + terms, None)
    initial = jnp.zeros((SUBGRIDS, ROWS, 2 * POINTS), jnp.float32)
    summed, _ = lax.scan(accumulate, initial, jnp.arange(N_FACET, dtype=jnp.int32))
    subgrids = summed.astype(jnp.bfloat16)
    slot_ids, is_held = slot_layout(offsets * 0 + owner.astype(jnp.int32), SLOTS, SLOT_TOTAL)
    grids = jnp.take(subgrids, slot_ids, axis=0)
    block = min(1024, VIS)

    def degrid_one(inputs):
        grid, obs_slot, coords, live_count, held_flag = inputs
        return degrid_slot(grid, obs_slot, coords, live_count, held_flag, block, POINTS, matmul)
    updates, residual_vis = lax.map(degrid_one, (grids, observed, vis_uv, vis_count.astype(jnp.int32), is_held))

    def facet_image(facet):
        return lift_back(updates, slot_ids, offsets, facet * FACET_WIDTH, phase_table, modulus, POINTS, matmul)
    images = lax.map(facet_image, jnp.arange(N_FACET, dtype=jnp.int32))
    weight = jnp.concatenate([prolate, prolate]) / math.sqrt(SUBGRIDS * POINTS)
    images = images * weight
    image_update = images.reshape(N_FACET, ROWS, 2, FACET_WIDTH).transpose(2, 1, 0, 3).reshape(2, ROWS, modulus)
    return (residual_vis, image_update)
```

```python
import functools
import math

import jax
import jax.numpy as jnp
import numpy as np
from jax import lax
from jax.experimental import pallas as pl
from jax.experimental.pallas import tpu as pltpu
from jax.sharding import PartitionSpec as P

POINTS = 512
FINE = 128
COARSE = POINTS // FINE
CHUNK = 512
TWO_PI = 6.283185307179586
SIN = [(-1) ** k * math.pi ** (2 * k + 1) / math.factorial(2 * k + 1) for k in range(7)]
COS = [(-1) ** k * math.pi ** (2 * k) / math.factorial(2 * k) for k in range(7)]


def sincos_turns(turns):
    frac = turns - jnp.floor(turns + 0.5)
    square = frac * frac
    sine = jnp.full_like(square, SIN[-1])
    cosine = jnp.full_like(square, COS[-1])
    for k in range(len(SIN) - 2, -1, -1):
        sine = sine * square + SIN[k]
        cosine = cosine * square + COS[k]
    sine = sine * frac
    return 1.0 - 2.0 * sine * sine, 2.0 * sine * cosine


def mod(value, modulus):
    if modulus & (modulus - 1) == 0:
        return value & (modulus - 1)
    return lax.rem(value, jnp.int32(modulus))


def wide_table(width, points, modulus):
    index = (np.arange(width, dtype=np.int64)[:, None] * np.arange(points)[None, :]) % modulus
    angle = index.astype(np.float32) * np.float32(TWO_PI / modulus)
    return np.concatenate([np.cos(angle), np.sin(angle)], 1)


def iota(shape, dim):
    return lax.broadcasted_iota(jnp.int32, shape, dim)


def slot_scalars(owner, slots):
    count = owner.shape[0]
    names = [owner[s] for s in range(count)]
    found = []
    for s in range(count):
        rank = jnp.int32(0)
        for before in range(s):
            rank = rank + jnp.where(names[before] == names[s], 1, 0)
        found.append(names[s] * slots + rank)
    return found


def build_tables(uv, fine, coarse_cos, coarse_sin):
    slots, total = uv.shape
    for q in range(slots):

        def visit(c, carry):
            where = pl.ds(pl.multiple_of(c * CHUNK, CHUNK), CHUNK)
            turn = jnp.broadcast_to(uv[pl.ds(q, 1), where], (8, CHUNK)) * (1.0 / POINTS)
            row = iota((8, CHUNK), 0)
            steps = jnp.where(
                row < 6, jnp.left_shift(8, jnp.minimum(row, 5)), jnp.where(row == 6, 384, 0)
            )
            base_cos, base_sin = sincos_turns(row.astype(jnp.float32) * turn)
            step_cos, step_sin = sincos_turns(steps.astype(jnp.float32) * turn)
            coarse_cos[q, :, where] = step_cos
            coarse_sin[q, :, where] = step_sin
            tiles = [(base_cos, base_sin)]
            for level in range(4):
                by_cos = step_cos[level : level + 1, :]
                by_sin = step_sin[level : level + 1, :]
                tiles = tiles + [
                    (a * by_cos - b * by_sin, a * by_sin + b * by_cos) for a, b in tiles
                ]
            for k in range(0, 16, 2):
                for part in range(2):
                    pair = jnp.concatenate([tiles[k][part], tiles[k + 1][part]], 0)
                    fine[q, pl.ds(part * FINE + k * 8, 16), where] = pair.astype(jnp.bfloat16)
            return carry

        lax.fori_loop(0, total // CHUNK, visit, 0)


def forward_slot(sky, prolate, offset, table, modulated, raw, turn_cos, turn_sin):
    facets = sky.shape[0]
    rows = sky.shape[2]
    width = sky.shape[3]
    modulus = facets * width
    index = mod(iota((8, width), 1) * offset, modulus)
    cosine, sine = sincos_turns(index.astype(jnp.float32) * (1.0 / modulus))
    cosine = cosine[:rows] * prolate[...]
    sine = sine[:rows] * prolate[...]

    def modulate(f, carry):
        real = sky[f, 0].astype(jnp.float32)
        imag = sky[f, 1].astype(jnp.float32)
        both = jnp.concatenate([real * cosine + imag * sine, imag * cosine - real * sine], 0)
        modulated[f] = both.astype(jnp.bfloat16)
        return carry

    lax.fori_loop(0, facets, modulate, 0)
    raw[...] = jnp.dot(
        modulated[...].reshape(facets * 2 * rows, width),
        table[...],
        preferred_element_type=jnp.float32,
    ).reshape(facets, 2 * rows, 2 * POINTS)
    place = mod(iota((facets, POINTS), 1) + offset, facets) * iota((facets, POINTS), 0)
    cosine, sine = sincos_turns(mod(place, facets).astype(jnp.float32) * (1.0 / facets))
    turn_cos[...] = cosine
    turn_sin[...] = sine

    def add(f, carry):
        sum_re, sum_im = carry
        upper = raw[f, :rows]
        lower = raw[f, rows:]
        real = upper[:, :POINTS] + lower[:, POINTS:]
        imag = lower[:, :POINTS] - upper[:, POINTS:]
        c = turn_cos[pl.ds(f, 1), :]
        s = turn_sin[pl.ds(f, 1), :]
        return sum_re + real * c + imag * s, sum_im + imag * c - real * s

    zero = jnp.zeros((rows, POINTS), jnp.float32)
    real, imag = lax.fori_loop(0, facets, add, (zero, zero))
    scale = 1.0 / math.sqrt(modulus)
    return real * scale, imag * scale


def degrid(q, grid_re, grid_im, live, observed, fine, coarse_cos, coarse_sin, residual):
    rows = grid_re.shape[0]
    total = observed.shape[3]
    parts_re, parts_im = [], []
    for a in range(COARSE):
        re = grid_re[:, a * FINE : (a + 1) * FINE]
        im = grid_im[:, a * FINE : (a + 1) * FINE]
        parts_re.append(jnp.concatenate([re, -im], 1))
        parts_im.append(jnp.concatenate([im, re], 1))
    left = jnp.concatenate(parts_re + parts_im, 0).astype(jnp.bfloat16)
    half = COARSE * rows
    scale = 1.0 / math.sqrt(POINTS)

    def visit(c, carry):
        start = pl.multiple_of(c * CHUNK, CHUNK)
        where = pl.ds(start, CHUNK)
        basis = fine[q, :, where]
        inner = jnp.dot(left, basis, preferred_element_type=jnp.float32)
        model_re = inner[:rows]
        model_im = inner[half : half + rows]
        turns = []
        for a in range(1, COARSE):
            ec = coarse_cos[q, pl.ds(3 + a, 1), where]
            es = coarse_sin[q, pl.ds(3 + a, 1), where]
            turns.append((ec, es))
            re = inner[a * rows : (a + 1) * rows]
            im = inner[half + a * rows : half + (a + 1) * rows]
            model_re = model_re + re * ec - im * es
            model_im = model_im + re * es + im * ec
        alive = iota((rows, CHUNK), 1) + start < live
        res_re = jnp.where(alive, observed[q, 0, :, where] - model_re * scale, 0.0)
        res_im = jnp.where(alive, observed[q, 1, :, where] - model_im * scale, 0.0)
        res_re = res_re.astype(jnp.bfloat16)
        res_im = res_im.astype(jnp.bfloat16)
        residual[q, 0, :, where] = res_re
        residual[q, 1, :, where] = res_im
        res_re = res_re.astype(jnp.float32)
        res_im = res_im.astype(jnp.float32)
        back_re, back_im = [res_re], [res_im]
        for ec, es in turns:
            back_re.append(res_re * ec + res_im * es)
            back_im.append(res_im * ec - res_re * es)
        back = jnp.concatenate(back_re + back_im, 0).astype(jnp.bfloat16)
        return carry + lax.dot_general(
            back, basis, (((1,), (1,)), ((), ())), preferred_element_type=jnp.float32
        )

    found = lax.fori_loop(
        0, total // CHUNK, visit, jnp.zeros((2 * half, 2 * FINE), jnp.float32)
    )
    upper, lower = found[:half], found[half:]
    real = upper[:, :FINE] + lower[:, FINE:]
    imag = lower[:, :FINE] - upper[:, FINE:]
    real = jnp.concatenate([real[a * rows : (a + 1) * rows] for a in range(COARSE)], 1)
    imag = jnp.concatenate([imag[a * rows : (a + 1) * rows] for a in range(COARSE)], 1)
    return jnp.concatenate([real, imag], 0) * (1.0 / math.sqrt(total))


def middle_kernel(
    offsets, owner, counts, sky, prolate, table, observed, uv, residual, update,
    fine, coarse_cos, coarse_sin, modulated, raw, turn_cos, turn_sin,
):
    slots = observed.shape[0]
    me = lax.axis_index("facet")
    build_tables(uv, fine, coarse_cos, coarse_sin)
    found = slot_scalars(owner, slots)
    for q in range(slots):
        offset = jnp.int32(0)
        live = jnp.int32(0)
        for s, slot in enumerate(found):
            here = slot == me * slots + q
            offset = jnp.where(here, offsets[s], offset)
            live = jnp.where(here, counts[q], live)
        real, imag = forward_slot(
            sky, prolate, offset, table, modulated, raw, turn_cos, turn_sin
        )
        result = degrid(
            q, real, imag, live, observed, fine, coarse_cos, coarse_sin, residual
        )
        update[q] = result.astype(jnp.bfloat16)


def lift(me, facets, offsets, owner, prolate, table, updates, image, scratch):
    lifted, back_cos, back_sin, turn_cos, turn_sin, across_cos, across_sin = scratch
    slots = updates.shape[1]
    number = facets * slots
    rows = updates.shape[2] // 2
    width = table.shape[0]
    modulus = width * facets
    found = slot_scalars(owner, slots)
    chosen = jnp.zeros((number, POINTS), jnp.int32)
    row = iota((number, POINTS), 0)
    for s, slot in enumerate(found):
        chosen = jnp.where(row == slot, offsets[s], chosen)
    place = mod(mod(iota((number, POINTS), 1) + chosen, facets) * me, facets)
    turn_cos[...], turn_sin[...] = sincos_turns(place.astype(jnp.float32) * (1.0 / facets))
    for start in range(0, width, POINTS):
        index = mod((iota((number, POINTS), 1) + start) * chosen, modulus)
        cosine, sine = sincos_turns(index.astype(jnp.float32) * (1.0 / modulus))
        across_cos[:, start : start + POINTS] = cosine
        across_sin[:, start : start + POINTS] = sine

    def raise_one(f, carry):
        for q in range(slots):
            at = f * slots + q
            piece = updates[f, q].astype(jnp.float32)
            real, imag = piece[:rows], piece[rows:]
            c = turn_cos[pl.ds(at, 1), :]
            s = turn_sin[pl.ds(at, 1), :]
            both = jnp.concatenate([real * c - imag * s, real * s + imag * c], 0)
            lifted[at] = both.astype(jnp.bfloat16)
        return carry

    lax.fori_loop(0, facets, raise_one, 0)
    left = lifted[...].reshape(number * 2 * rows, POINTS)
    contract = (((1,), (1,)), ((), ()))
    for target, begin in ((back_cos, 0), (back_sin, POINTS)):
        target[...] = lax.dot_general(
            left,
            table[:, begin : begin + POINTS],
            contract,
            preferred_element_type=jnp.float32,
        ).reshape(number, 2 * rows, width)

    def add(at, carry):
        sum_re, sum_im = carry
        real = back_cos[at, :rows] - back_sin[at, rows:]
        imag = back_sin[at, :rows] + back_cos[at, rows:]
        c = across_cos[pl.ds(at, 1), :]
        s = across_sin[pl.ds(at, 1), :]
        return sum_re + real * c - imag * s, sum_im + real * s + imag * c

    zero = jnp.zeros((rows, width), jnp.float32)
    sum_re, sum_im = lax.fori_loop(0, number, add, (zero, zero))
    weight = prolate[...] * (1.0 / math.sqrt(offsets.shape[0] * POINTS))
    image[0] = sum_re * weight
    image[1] = sum_im * weight


def lift_kernel(offsets, owner, prolate, table, updates, image, *scratch):
    lift(
        lax.axis_index("facet"), updates.shape[0], offsets, owner, prolate, table, updates,
        image, scratch,
    )


VMEM = pl.BlockSpec(memory_space=pltpu.VMEM)
SMEM = pl.BlockSpec(memory_space=pltpu.SMEM)


def local(sky_strips, prolate, subgrid_offset, owner, observed, vis_uv, vis_count):
    rows, width = sky_strips.shape[1:]
    facets = lax.axis_size("facet")
    slots, _, _, total = observed.shape
    number = facets * slots
    table = jnp.asarray(wide_table(width, POINTS, width * facets), jnp.bfloat16)
    prolate_row = prolate[None, :]
    params = pltpu.CompilerParams(vmem_limit_bytes=56 * 1024 * 1024)
    f32, bf16 = jnp.float32, jnp.bfloat16
    sky = lax.all_gather(sky_strips, "facet", axis=0)
    residual, update = pl.pallas_call(
        middle_kernel,
        out_shape=(
            jax.ShapeDtypeStruct(observed.shape, bf16),
            jax.ShapeDtypeStruct((slots, 2 * rows, POINTS), bf16),
        ),
        in_specs=[SMEM] * 3 + [VMEM] * 5,
        out_specs=(VMEM, VMEM),
        scratch_shapes=[
            pltpu.VMEM((slots, 2 * FINE, total), bf16),
            pltpu.VMEM((slots, 8, total), f32),
            pltpu.VMEM((slots, 8, total), f32),
            pltpu.VMEM((facets, 2 * rows, width), bf16),
            pltpu.VMEM((facets, 2 * rows, 2 * POINTS), f32),
            pltpu.VMEM((facets, POINTS), f32),
            pltpu.VMEM((facets, POINTS), f32),
        ],
        compiler_params=params,
    )(subgrid_offset, owner, vis_count, sky, prolate_row, table, observed, vis_uv)
    updates = lax.all_gather(update, "facet", axis=0)
    image = pl.pallas_call(
        lift_kernel,
        out_shape=jax.ShapeDtypeStruct((2, rows, width), f32),
        in_specs=[SMEM] * 2 + [VMEM] * 3,
        out_specs=VMEM,
        scratch_shapes=[
            pltpu.VMEM((number, 2 * rows, POINTS), bf16),
            pltpu.VMEM((number, 2 * rows, width), f32),
            pltpu.VMEM((number, 2 * rows, width), f32),
            pltpu.VMEM((number, POINTS), f32),
            pltpu.VMEM((number, POINTS), f32),
            pltpu.VMEM((number, width), f32),
            pltpu.VMEM((number, width), f32),
        ],
        compiler_params=params,
    )(subgrid_offset, owner, prolate_row, table, updates)
    return residual, image


def solution(mesh):
    in_specs = (
        P(None, "groups", "facet"),
        P(),
        P(),
        P(),
        P(("groups", "facet"), None, None, None),
        P(("groups", "facet"), None),
        P(("groups", "facet")),
    )
    out_specs = (P(("groups", "facet"), None, None, None), P(None, "groups", "facet"))
    return jax.shard_map(local, mesh=mesh, in_specs=in_specs, out_specs=out_specs, check_vma=False)
```

```python
import math

import jax
import jax.numpy as jnp
import numpy as np
from jax import lax
from jax.experimental import pallas as pl
from jax.experimental.pallas import tpu as pltpu
from jax.sharding import PartitionSpec as P

POINTS = 512
FINE = 128
COARSE = POINTS // FINE
CHUNK = 512
TWO_PI = 6.283185307179586
SIN = [(-1) ** k * math.pi ** (2 * k + 1) / math.factorial(2 * k + 1) for k in range(7)]
COS = [(-1) ** k * math.pi ** (2 * k) / math.factorial(2 * k) for k in range(7)]


def sincos_turns(turns):
    frac = turns - jnp.floor(turns + 0.5)
    square = frac * frac
    sine = jnp.full_like(square, SIN[-1])
    cosine = jnp.full_like(square, COS[-1])
    for k in range(len(SIN) - 2, -1, -1):
        sine = sine * square + SIN[k]
        cosine = cosine * square + COS[k]
    sine = sine * frac
    return 1.0 - 2.0 * sine * sine, 2.0 * sine * cosine


def mod(value, modulus):
    if modulus & (modulus - 1) == 0:
        return value & (modulus - 1)
    return lax.rem(value, jnp.int32(modulus))


def wide_table(width, points, modulus):
    index = (np.arange(width, dtype=np.int64)[:, None] * np.arange(points)[None, :]) % modulus
    angle = index.astype(np.float32) * np.float32(TWO_PI / modulus)
    return np.concatenate([np.cos(angle), np.sin(angle)], 1)


def iota(shape, dim):
    return lax.broadcasted_iota(jnp.int32, shape, dim)


def slot_scalars(owner, slots):
    count = owner.shape[0]
    names = [owner[s] for s in range(count)]
    found = []
    for s in range(count):
        rank = jnp.int32(0)
        for before in range(s):
            rank = rank + jnp.where(names[before] == names[s], 1, 0)
        found.append(names[s] * slots + rank)
    return found


def build_tables(q, uv, fine, coarse_cos, coarse_sin):
    total = uv.shape[1]

    def visit(c, carry):
        where = pl.ds(pl.multiple_of(c * CHUNK, CHUNK), CHUNK)
        turn = jnp.broadcast_to(uv[pl.ds(q, 1), where], (8, CHUNK)) * (1.0 / POINTS)
        row = iota((8, CHUNK), 0)
        steps = jnp.where(
            row < 6, jnp.left_shift(8, jnp.minimum(row, 5)), jnp.where(row == 6, 384, 0)
        )
        base_cos, base_sin = sincos_turns(row.astype(jnp.float32) * turn)
        step_cos, step_sin = sincos_turns(steps.astype(jnp.float32) * turn)
        coarse_cos[q, :, where] = step_cos
        coarse_sin[q, :, where] = step_sin
        tiles = [(base_cos, base_sin)]
        for level in range(4):
            by_cos = step_cos[level : level + 1, :]
            by_sin = step_sin[level : level + 1, :]
            tiles = tiles + [
                (a * by_cos - b * by_sin, a * by_sin + b * by_cos) for a, b in tiles
            ]
        for k in range(0, 16, 2):
            for part in range(2):
                pair = jnp.concatenate([tiles[k][part], tiles[k + 1][part]], 0)
                fine[q, pl.ds(part * FINE + k * 8, 16), where] = pair.astype(jnp.bfloat16)
        return carry

    lax.fori_loop(0, total // CHUNK, visit, 0)


def forward_slot(sky, prolate, offset, table, modulated, raw, turn_cos, turn_sin):
    facets = sky.shape[0]
    rows = sky.shape[1] // 2
    width = sky.shape[2]
    modulus = facets * width
    index = mod(iota((8, width), 1) * offset, modulus)
    cosine, sine = sincos_turns(index.astype(jnp.float32) * (1.0 / modulus))
    cosine = cosine[:rows] * prolate[...]
    sine = sine[:rows] * prolate[...]

    def modulate(f, carry):
        strip = sky[f].astype(jnp.float32)
        real, imag = strip[:rows], strip[rows:]
        both = jnp.concatenate([real * cosine + imag * sine, imag * cosine - real * sine], 0)
        modulated[f] = both.astype(jnp.bfloat16)
        return carry

    lax.fori_loop(0, facets, modulate, 0)
    raw[...] = jnp.dot(
        modulated[...].reshape(facets * 2 * rows, width),
        table[...],
        preferred_element_type=jnp.float32,
    ).reshape(facets, 2 * rows, 2 * POINTS)
    place = mod(iota((facets, POINTS), 1) + offset, facets) * iota((facets, POINTS), 0)
    cosine, sine = sincos_turns(mod(place, facets).astype(jnp.float32) * (1.0 / facets))
    turn_cos[...] = cosine
    turn_sin[...] = sine

    def add(f, carry):
        sum_re, sum_im = carry
        upper = raw[f, :rows]
        lower = raw[f, rows:]
        real = upper[:, :POINTS] + lower[:, POINTS:]
        imag = lower[:, :POINTS] - upper[:, POINTS:]
        c = turn_cos[pl.ds(f, 1), :]
        s = turn_sin[pl.ds(f, 1), :]
        return sum_re + real * c + imag * s, sum_im + imag * c - real * s

    zero = jnp.zeros((rows, POINTS), jnp.float32)
    real, imag = lax.fori_loop(0, facets, add, (zero, zero))
    scale = 1.0 / math.sqrt(modulus)
    return real * scale, imag * scale


def degrid(q, grid_re, grid_im, live, observed, fine, coarse_cos, coarse_sin, residual, midway):
    rows = grid_re.shape[0]
    total = observed.shape[3]
    parts_re, parts_im = [], []
    for a in range(COARSE):
        re = grid_re[:, a * FINE : (a + 1) * FINE]
        im = grid_im[:, a * FINE : (a + 1) * FINE]
        parts_re.append(jnp.concatenate([re, -im], 1))
        parts_im.append(jnp.concatenate([im, re], 1))
    left = jnp.concatenate(parts_re + parts_im, 0).astype(jnp.bfloat16)
    half = COARSE * rows
    scale = 1.0 / math.sqrt(POINTS)

    def visit(c, carry):
        start = pl.multiple_of(c * CHUNK, CHUNK)
        where = pl.ds(start, CHUNK)
        basis = fine[q, :, where]
        inner = jnp.dot(left, basis, preferred_element_type=jnp.float32)
        model_re = inner[:rows]
        model_im = inner[half : half + rows]
        turns = []
        for a in range(1, COARSE):
            ec = coarse_cos[q, pl.ds(3 + a, 1), where]
            es = coarse_sin[q, pl.ds(3 + a, 1), where]
            turns.append((ec, es))
            re = inner[a * rows : (a + 1) * rows]
            im = inner[half + a * rows : half + (a + 1) * rows]
            model_re = model_re + re * ec - im * es
            model_im = model_im + re * es + im * ec
        alive = iota((rows, CHUNK), 1) + start < live
        res_re = jnp.where(alive, observed[q, 0, :, where] - model_re * scale, 0.0)
        res_im = jnp.where(alive, observed[q, 1, :, where] - model_im * scale, 0.0)
        rounded = jnp.concatenate([res_re, res_im], 0).astype(jnp.bfloat16)
        residual[q, :, where] = rounded
        rounded = rounded.astype(jnp.float32)
        res_re, res_im = rounded[:rows], rounded[rows:]
        back_re, back_im = [res_re], [res_im]
        for ec, es in turns:
            back_re.append(res_re * ec + res_im * es)
            back_im.append(res_im * ec - res_re * es)
        back = jnp.concatenate(back_re + back_im, 0).astype(jnp.bfloat16)
        return carry + lax.dot_general(
            back, basis, (((1,), (1,)), ((), ())), preferred_element_type=jnp.float32
        )

    steps = total // CHUNK
    found = jnp.zeros((2 * half, 2 * FINE), jnp.float32)
    found = lax.fori_loop(0, steps // 2, visit, found)
    midway()
    found = lax.fori_loop(steps // 2, steps, visit, found)
    upper, lower = found[:half], found[half:]
    real = upper[:, :FINE] + lower[:, FINE:]
    imag = lower[:, :FINE] - upper[:, FINE:]
    real = jnp.concatenate([real[a * rows : (a + 1) * rows] for a in range(COARSE)], 1)
    imag = jnp.concatenate([imag[a * rows : (a + 1) * rows] for a in range(COARSE)], 1)
    return jnp.concatenate([real, imag], 0) * (1.0 / math.sqrt(total))


class Gather:
    def __init__(self, held, send, recv):
        self.held, self.send, self.recv = held, send, recv
        self.facets = held.shape[0]
        self.outer = self.facets // 4
        self.me = lax.axis_index("facet")
        self.z = lax.div(self.me, 4)
        self.y = lax.rem(lax.div(self.me, 2), 2)
        self.c = lax.rem(self.me, 2)
        self.sent = []

    def name(self, step, row, core):
        return lax.rem(self.z + step, self.outer) * 4 + row * 2 + core

    def peers(self):
        along = [self.name(step, self.y, self.c) for step in range(1, self.outer)]
        return along + [self.name(0, 1 - self.y, self.c), self.name(0, self.y, 1 - self.c)]

    def copy(self, block, sem, target):
        return pltpu.make_async_remote_copy(
            src_ref=self.held.at[block],
            dst_ref=self.held.at[block],
            send_sem=sem,
            recv_sem=self.recv.at[block],
            device_id={"facet": target},
            device_id_type=pl.DeviceIdType.MESH,
        )

    def push(self, block, sem, target):
        copy = self.copy(block, sem, target)
        copy.start()
        self.sent.append(copy)

    def arrive(self, block):
        self.copy(block, self.send.at[0, 0], self.me).wait_recv()

    def to_row(self, block):
        self.push(block, self.send.at[1, block], self.name(0, 1 - self.y, self.c))

    def to_core(self, block):
        self.push(block, self.send.at[2, block], self.name(0, self.y, 1 - self.c))

    def start(self):
        for step in range(1, self.outer):
            self.push(self.me, self.send.at[0, step], self.name(step, self.y, self.c))
        self.to_row(self.me)
        self.to_core(self.me)

    def relay_first(self):
        for step in range(self.outer - 1, 0, -1):
            block = self.name(step, self.y, self.c)
            self.arrive(block)
            self.to_row(block)
            self.to_core(block)

    def relay_second(self):
        for step in range(self.outer, 0, -1):
            block = self.name(step, 1 - self.y, self.c)
            self.arrive(block)
            self.to_core(block)

    def finish(self):
        for row in range(2):
            for step in range(self.outer, 0, -1):
                self.arrive(self.name(step, row, 1 - self.c))

    def drain(self):
        for copy in self.sent:
            copy.wait_send()


def lift_slot(q, slots, offsets, found, updates, table, before, scratch):
    lifted, back_cos, back_sin, turn_cos, turn_sin, across_cos, across_sin = scratch
    facets, both, _ = lifted.shape
    rows = both // 2
    width = table.shape[0]
    modulus = width * facets
    me = lax.axis_index("facet")
    chosen = jnp.zeros((facets, POINTS), jnp.int32)
    row = iota((facets, POINTS), 0) * slots + q
    for s, slot in enumerate(found):
        chosen = jnp.where(row == slot, offsets[s], chosen)
    place = mod(mod(iota((facets, POINTS), 1) + chosen, facets) * me, facets)
    turn_cos[...], turn_sin[...] = sincos_turns(place.astype(jnp.float32) * (1.0 / facets))
    for start in range(0, width, POINTS):
        index = mod((iota((facets, POINTS), 1) + start) * chosen, modulus)
        cosine, sine = sincos_turns(index.astype(jnp.float32) * (1.0 / modulus))
        across_cos[:, start : start + POINTS] = cosine
        across_sin[:, start : start + POINTS] = sine
    before()

    def raise_one(f, carry):
        piece = updates[f].astype(jnp.float32)
        real, imag = piece[:rows], piece[rows:]
        c = turn_cos[pl.ds(f, 1), :]
        s = turn_sin[pl.ds(f, 1), :]
        lifted[f] = jnp.concatenate([real * c - imag * s, real * s + imag * c], 0).astype(
            jnp.bfloat16
        )
        return carry

    lax.fori_loop(0, facets, raise_one, 0)
    left = lifted[...].reshape(facets * both, POINTS)
    for target, begin in ((back_cos, 0), (back_sin, POINTS)):
        target[...] = lax.dot_general(
            left,
            table[:, begin : begin + POINTS],
            (((1,), (1,)), ((), ())),
            preferred_element_type=jnp.float32,
        ).reshape(facets, both, width)

    def add(f, carry):
        sum_re, sum_im = carry
        real = back_cos[f, :rows] - back_sin[f, rows:]
        imag = back_sin[f, :rows] + back_cos[f, rows:]
        c = across_cos[pl.ds(f, 1), :]
        s = across_sin[pl.ds(f, 1), :]
        return sum_re + real * c - imag * s, sum_im + real * s + imag * c

    zero = jnp.zeros((rows, width), jnp.float32)
    return lax.fori_loop(0, facets, add, (zero, zero))


def whole_kernel(
    offsets, owner, counts, sky_own, prolate, table_far, observed_far, uv,
    residual_far, image,
    sky, updates, table, observed, residual, fine, coarse_cos, coarse_sin, modulated, raw,
    turn_cos, turn_sin, lifted, back_cos, back_sin, across_cos, across_sin,
    sky_send, sky_recv, update_send, update_recv, local_sem,
):
    slots = observed.shape[0]
    me = lax.axis_index("facet")
    gather = Gather(sky, sky_send, sky_recv)
    back = [
        Gather(updates.at[q], update_send.at[q], update_recv.at[q]) for q in range(slots)
    ]
    load_table = pltpu.make_async_copy(table_far, table, local_sem.at[0])
    load_table.start()
    loads = [
        pltpu.make_async_copy(observed_far.at[q], observed.at[q], local_sem.at[1 + q])
        for q in range(slots)
    ]
    for load in loads:
        load.start()
    barrier = pltpu.get_barrier_semaphore()
    peers = gather.peers()
    for peer in peers:
        pl.semaphore_signal(
            barrier, inc=1, device_id={"facet": peer}, device_id_type=pl.DeviceIdType.MESH
        )
    sky[me] = sky_own[...]
    pl.semaphore_wait(barrier, len(peers))
    gather.start()
    for q in range(slots):
        build_tables(q, uv, fine, coarse_cos, coarse_sin)
        if q == 0:
            gather.relay_first()
        if q == slots - 1:
            gather.relay_second()
    found = slot_scalars(owner, slots)
    load_table.wait()
    gather.finish()
    stores = []
    for q in range(slots):
        offset = jnp.int32(0)
        live = jnp.int32(0)
        for s, slot in enumerate(found):
            here = slot == me * slots + q
            offset = jnp.where(here, offsets[s], offset)
            live = jnp.where(here, counts[q], live)
        real, imag = forward_slot(
            sky, prolate, offset, table, modulated, raw, turn_cos, turn_sin
        )
        if q > 0:
            back[q - 1].relay_first()
        loads[q].wait()
        result = degrid(
            q, real, imag, live, observed, fine, coarse_cos, coarse_sin, residual,
            back[q - 1].relay_second if q > 0 else lambda: None,
        )
        updates[q, me] = result.astype(jnp.bfloat16)
        back[q].start()
        store = pltpu.make_async_copy(residual.at[q], residual_far.at[q], local_sem.at[1 + slots + q])
        store.start()
        stores.append(store)
    scratch = (lifted, back_cos, back_sin, turn_cos, turn_sin, across_cos, across_sin)
    last = back[slots - 1]
    sum_re = sum_im = 0.0
    for q in range(slots):

        def before():
            if q == 0:
                last.relay_first()
            if q == slots - 1:
                last.relay_second()
            back[q].finish()

        part_re, part_im = lift_slot(
            q, slots, offsets, found, updates.at[q], table, before, scratch
        )
        sum_re = sum_re + part_re
        sum_im = sum_im + part_im
    weight = prolate[...] * (1.0 / math.sqrt(offsets.shape[0] * POINTS))
    image[0] = sum_re * weight
    image[1] = sum_im * weight
    gather.drain()
    for one in back:
        one.drain()
    for store in stores:
        store.wait()


VMEM = pl.BlockSpec(memory_space=pltpu.VMEM)
SMEM = pl.BlockSpec(memory_space=pltpu.SMEM)
FAR = pl.BlockSpec(memory_space=pl.ANY)


def local(sky_strips, prolate, subgrid_offset, owner, observed, vis_uv, vis_count):
    rows, width = sky_strips.shape[1:]
    facets = lax.axis_size("facet")
    slots, _, _, total = observed.shape
    both = 2 * rows
    table = jnp.asarray(wide_table(width, POINTS, width * facets), jnp.bfloat16)
    f32, bf16 = jnp.float32, jnp.bfloat16
    residual, image = pl.pallas_call(
        whole_kernel,
        out_shape=(
            jax.ShapeDtypeStruct((slots, both, total), bf16),
            jax.ShapeDtypeStruct((2, rows, width), f32),
        ),
        in_specs=[SMEM] * 3 + [VMEM] * 2 + [FAR] * 2 + [VMEM],
        out_specs=(FAR, VMEM),
        scratch_shapes=[
            pltpu.VMEM((facets, both, width), bf16),
            pltpu.VMEM((slots, facets, both, POINTS), bf16),
            pltpu.VMEM(table.shape, bf16),
            pltpu.VMEM(observed.shape, f32),
            pltpu.VMEM((slots, both, total), bf16),
            pltpu.VMEM((slots, 2 * FINE, total), bf16),
            pltpu.VMEM((slots, 8, total), f32),
            pltpu.VMEM((slots, 8, total), f32),
            pltpu.VMEM((facets, both, width), bf16),
            pltpu.VMEM((facets, both, 2 * POINTS), f32),
            pltpu.VMEM((facets, POINTS), f32),
            pltpu.VMEM((facets, POINTS), f32),
            pltpu.VMEM((facets, both, POINTS), bf16),
            pltpu.VMEM((facets, both, width), f32),
            pltpu.VMEM((facets, both, width), f32),
            pltpu.VMEM((facets, width), f32),
            pltpu.VMEM((facets, width), f32),
            pltpu.SemaphoreType.DMA((3, facets)),
            pltpu.SemaphoreType.DMA((facets,)),
            pltpu.SemaphoreType.DMA((slots, 3, facets)),
            pltpu.SemaphoreType.DMA((slots, facets)),
            pltpu.SemaphoreType.DMA((1 + 2 * slots,)),
        ],
        compiler_params=pltpu.CompilerParams(
            collective_id=0, has_side_effects=True, vmem_limit_bytes=56 * 1024 * 1024
        ),
    )(
        subgrid_offset,
        owner,
        vis_count,
        sky_strips.reshape(both, width),
        prolate[None, :],
        table,
        observed,
        vis_uv,
    )
    return residual.reshape(slots, 2, rows, total), image


def solution(mesh):
    in_specs = (
        P(None, "groups", "facet"),
        P(),
        P(),
        P(),
        P(("groups", "facet"), None, None, None),
        P(("groups", "facet"), None),
        P(("groups", "facet")),
    )
    out_specs = (P(("groups", "facet"), None, None, None), P(None, "groups", "facet"))
    return jax.shard_map(local, mesh=mesh, in_specs=in_specs, out_specs=out_specs, check_vma=False)
```

```python
import functools
import math

import jax
import jax.numpy as jnp
import numpy as np
from jax import lax
from jax.experimental import pallas as pl
from jax.experimental.pallas import tpu as pltpu
from jax.sharding import PartitionSpec as P

POINTS = 512
FINE = 128
COARSE = POINTS // FINE
CHUNK = 1024
UNROLL = 4
TWO_PI = 6.283185307179586
SIN = [(-1) ** k * math.pi ** (2 * k + 1) / math.factorial(2 * k + 1) for k in range(7)]
COS = [(-1) ** k * math.pi ** (2 * k) / math.factorial(2 * k) for k in range(7)]


def sincos_turns(turns):
    frac = turns - jnp.floor(turns + 0.5)
    square = frac * frac
    sine = jnp.full_like(square, SIN[-1])
    cosine = jnp.full_like(square, COS[-1])
    for k in range(len(SIN) - 2, -1, -1):
        sine = sine * square + SIN[k]
        cosine = cosine * square + COS[k]
    sine = sine * frac
    return 1.0 - 2.0 * sine * sine, 2.0 * sine * cosine


def mod(value, modulus):
    if modulus & (modulus - 1) == 0:
        return value & (modulus - 1)
    return lax.rem(value, jnp.int32(modulus))


def wide_table(width, points, modulus):
    index = (np.arange(width, dtype=np.int64)[:, None] * np.arange(points)[None, :]) % modulus
    angle = index.astype(np.float32) * np.float32(TWO_PI / modulus)
    return np.concatenate([np.cos(angle), np.sin(angle)], 1)


def iota(shape, dim):
    return lax.broadcasted_iota(jnp.int32, shape, dim)


def slot_scalars(owner, slots):
    count = owner.shape[0]
    names = [owner[s] for s in range(count)]
    found = []
    for s in range(count):
        rank = jnp.int32(0)
        for before in range(s):
            rank = rank + jnp.where(names[before] == names[s], 1, 0)
        found.append(names[s] * slots + rank)
    return found


def build_tables(q, uv, fine, coarse_cos, coarse_sin):
    total = uv.shape[1]

    def visit(c, carry):
        where = pl.ds(pl.multiple_of(c * CHUNK, CHUNK), CHUNK)
        turn = jnp.broadcast_to(uv[pl.ds(q, 1), where], (8, CHUNK)) * (1.0 / POINTS)
        row = iota((8, CHUNK), 0)
        steps = jnp.where(
            row < 6, jnp.left_shift(8, jnp.minimum(row, 5)), jnp.where(row == 6, 384, 0)
        )
        base_cos, base_sin = sincos_turns(row.astype(jnp.float32) * turn)
        step_cos, step_sin = sincos_turns(steps.astype(jnp.float32) * turn)
        coarse_cos[q, :, where] = step_cos
        coarse_sin[q, :, where] = step_sin
        tiles = [(base_cos, base_sin)]
        for level in range(4):
            by_cos = step_cos[level : level + 1, :]
            by_sin = step_sin[level : level + 1, :]
            tiles = tiles + [
                (a * by_cos - b * by_sin, a * by_sin + b * by_cos) for a, b in tiles
            ]
        for k in range(0, 16, 2):
            for part in range(2):
                pair = jnp.concatenate([tiles[k][part], tiles[k + 1][part]], 0)
                fine[q, pl.ds(part * FINE + k * 8, 16), where] = pair.astype(jnp.bfloat16)
        return carry

    lax.fori_loop(0, total // CHUNK, visit, 0)


def forward_slot(sky, prolate, offset, table, modulated, raw, turn_cos, turn_sin):
    facets = sky.shape[0]
    rows = sky.shape[1] // 2
    width = sky.shape[2]
    modulus = facets * width
    index = mod(iota((8, width), 1) * offset, modulus)
    cosine, sine = sincos_turns(index.astype(jnp.float32) * (1.0 / modulus))
    cosine = cosine[:rows] * prolate[...]
    sine = sine[:rows] * prolate[...]

    def modulate(f, carry):
        strip = sky[f].astype(jnp.float32)
        real, imag = strip[:rows], strip[rows:]
        both = jnp.concatenate([real * cosine + imag * sine, imag * cosine - real * sine], 0)
        modulated[f] = both.astype(jnp.bfloat16)
        return carry

    lax.fori_loop(0, facets, modulate, 0, unroll=4)
    raw[...] = jnp.dot(
        modulated[...].reshape(facets * 2 * rows, width),
        table[...],
        preferred_element_type=jnp.float32,
    ).reshape(facets, 2 * rows, 2 * POINTS)
    place = mod(iota((facets, POINTS), 1) + offset, facets) * iota((facets, POINTS), 0)
    cosine, sine = sincos_turns(mod(place, facets).astype(jnp.float32) * (1.0 / facets))
    turn_cos[...] = cosine
    turn_sin[...] = sine

    def add(f, carry):
        sum_re, sum_im = carry
        upper = raw[f, :rows]
        lower = raw[f, rows:]
        real = upper[:, :POINTS] + lower[:, POINTS:]
        imag = lower[:, :POINTS] - upper[:, POINTS:]
        c = turn_cos[pl.ds(f, 1), :]
        s = turn_sin[pl.ds(f, 1), :]
        return sum_re + real * c + imag * s, sum_im + imag * c - real * s

    zero = jnp.zeros((rows, POINTS), jnp.float32)
    real, imag = lax.fori_loop(0, facets, add, (zero, zero), unroll=4)
    scale = 1.0 / math.sqrt(modulus)
    return real * scale, imag * scale


def degrid(q, grid_re, grid_im, live, observed, fine, coarse_cos, coarse_sin, residual, midway):
    rows = grid_re.shape[0]
    total = observed.shape[3]
    parts_re, parts_im = [], []
    for a in range(COARSE):
        re = grid_re[:, a * FINE : (a + 1) * FINE]
        im = grid_im[:, a * FINE : (a + 1) * FINE]
        parts_re.append(jnp.concatenate([re, -im], 1))
        parts_im.append(jnp.concatenate([im, re], 1))
    left = jnp.concatenate(parts_re + parts_im, 0).astype(jnp.bfloat16)
    half = COARSE * rows
    scale = 1.0 / math.sqrt(POINTS)

    def visit(c, carry):
        start = pl.multiple_of(c * CHUNK, CHUNK)
        where = pl.ds(start, CHUNK)
        basis = fine[q, :, where]
        inner = jnp.dot(left, basis, preferred_element_type=jnp.float32)
        model_re = inner[:rows]
        model_im = inner[half : half + rows]
        turns = []
        for a in range(1, COARSE):
            ec = coarse_cos[q, pl.ds(3 + a, 1), where]
            es = coarse_sin[q, pl.ds(3 + a, 1), where]
            turns.append((ec, es))
            re = inner[a * rows : (a + 1) * rows]
            im = inner[half + a * rows : half + (a + 1) * rows]
            model_re = model_re + re * ec - im * es
            model_im = model_im + re * es + im * ec
        alive = iota((rows, CHUNK), 1) + start < live
        res_re = jnp.where(alive, observed[q, 0, :, where] - model_re * scale, 0.0)
        res_im = jnp.where(alive, observed[q, 1, :, where] - model_im * scale, 0.0)
        rounded = jnp.concatenate([res_re, res_im], 0).astype(jnp.bfloat16)
        residual[q, :, where] = rounded
        rounded = rounded.astype(jnp.float32)
        res_re, res_im = rounded[:rows], rounded[rows:]
        back_re, back_im = [res_re], [res_im]
        for ec, es in turns:
            back_re.append(res_re * ec + res_im * es)
            back_im.append(res_im * ec - res_re * es)
        back = jnp.concatenate(back_re + back_im, 0).astype(jnp.bfloat16)
        return carry + lax.dot_general(
            back, basis, (((1,), (1,)), ((), ())), preferred_element_type=jnp.float32
        )

    steps = total // CHUNK
    found = jnp.zeros((2 * half, 2 * FINE), jnp.float32)
    found = lax.fori_loop(0, steps // 2, visit, found, unroll=UNROLL)
    midway()
    found = lax.fori_loop(steps // 2, steps, visit, found, unroll=UNROLL)
    upper, lower = found[:half], found[half:]
    real = upper[:, :FINE] + lower[:, FINE:]
    imag = lower[:, :FINE] - upper[:, FINE:]
    real = jnp.concatenate([real[a * rows : (a + 1) * rows] for a in range(COARSE)], 1)
    imag = jnp.concatenate([imag[a * rows : (a + 1) * rows] for a in range(COARSE)], 1)
    return jnp.concatenate([real, imag], 0) * (1.0 / math.sqrt(total))


class Gather:
    def __init__(self, held, send, recv):
        self.held, self.send, self.recv = held, send, recv
        self.facets = held.shape[0]
        self.outer = self.facets // 4
        self.me = lax.axis_index("facet")
        self.z = lax.div(self.me, 4)
        self.y = lax.rem(lax.div(self.me, 2), 2)
        self.c = lax.rem(self.me, 2)
        self.sent = []

    def name(self, step, row, core):
        return lax.rem(self.z + step, self.outer) * 4 + row * 2 + core

    def peers(self):
        along = [self.name(step, self.y, self.c) for step in range(1, self.outer)]
        return along + [self.name(0, 1 - self.y, self.c), self.name(0, self.y, 1 - self.c)]

    def copy(self, block, sem, target):
        return pltpu.make_async_remote_copy(
            src_ref=self.held.at[block],
            dst_ref=self.held.at[block],
            send_sem=sem,
            recv_sem=self.recv.at[block],
            device_id={"facet": target},
            device_id_type=pl.DeviceIdType.MESH,
        )

    def push(self, block, sem, target):
        copy = self.copy(block, sem, target)
        copy.start()
        self.sent.append(copy)

    def arrive(self, block):
        self.copy(block, self.send.at[0, 0], self.me).wait_recv()

    def to_row(self, block):
        self.push(block, self.send.at[1, block], self.name(0, 1 - self.y, self.c))

    def to_core(self, block):
        self.push(block, self.send.at[2, block], self.name(0, self.y, 1 - self.c))

    def start(self):
        for step in range(1, self.outer):
            self.push(self.me, self.send.at[0, step], self.name(step, self.y, self.c))
        self.to_row(self.me)
        self.to_core(self.me)

    def relay_first(self):
        for step in range(self.outer - 1, 0, -1):
            block = self.name(step, self.y, self.c)
            self.arrive(block)
            self.to_row(block)
            self.to_core(block)

    def relay_second(self):
        for step in range(self.outer, 0, -1):
            block = self.name(step, 1 - self.y, self.c)
            self.arrive(block)
            self.to_core(block)

    def finish(self):
        for row in range(2):
            for step in range(self.outer, 0, -1):
                self.arrive(self.name(step, row, 1 - self.c))

    def drain(self):
        for copy in self.sent:
            copy.wait_send()


def lift_phases(q, slots, offsets, found, turn_cos, turn_sin, across_cos, across_sin):
    facets, width = across_cos.shape
    modulus = width * facets
    me = lax.axis_index("facet")
    chosen = jnp.zeros((facets, POINTS), jnp.int32)
    row = iota((facets, POINTS), 0) * slots + q
    for s, slot in enumerate(found):
        chosen = jnp.where(row == slot, offsets[s], chosen)
    place = mod(mod(iota((facets, POINTS), 1) + chosen, facets) * me, facets)
    turn_cos[...], turn_sin[...] = sincos_turns(place.astype(jnp.float32) * (1.0 / facets))
    for start in range(0, width, POINTS):
        index = mod((iota((facets, POINTS), 1) + start) * chosen, modulus)
        cosine, sine = sincos_turns(index.astype(jnp.float32) * (1.0 / modulus))
        across_cos[:, start : start + POINTS] = cosine
        across_sin[:, start : start + POINTS] = sine


def lift_slot(updates, table, before, scratch):
    lifted, back_cos, back_sin, turn_cos, turn_sin, across_cos, across_sin = scratch
    facets, both, _ = lifted.shape
    rows = both // 2
    width = table.shape[0]
    before()

    def raise_one(f, carry):
        piece = updates[f].astype(jnp.float32)
        real, imag = piece[:rows], piece[rows:]
        c = turn_cos[pl.ds(f, 1), :]
        s = turn_sin[pl.ds(f, 1), :]
        lifted[f] = jnp.concatenate([real * c - imag * s, real * s + imag * c], 0).astype(
            jnp.bfloat16
        )
        return carry

    lax.fori_loop(0, facets, raise_one, 0, unroll=4)
    left = lifted[...].reshape(facets * both, POINTS)
    for target, begin in ((back_cos, 0), (back_sin, POINTS)):
        target[...] = lax.dot_general(
            left,
            table[:, begin : begin + POINTS],
            (((1,), (1,)), ((), ())),
            preferred_element_type=jnp.float32,
        ).reshape(facets, both, width)

    def add(f, carry):
        sum_re, sum_im = carry
        real = back_cos[f, :rows] - back_sin[f, rows:]
        imag = back_sin[f, :rows] + back_cos[f, rows:]
        c = across_cos[pl.ds(f, 1), :]
        s = across_sin[pl.ds(f, 1), :]
        return sum_re + real * c - imag * s, sum_im + real * s + imag * c

    zero = jnp.zeros((rows, width), jnp.float32)
    return lax.fori_loop(0, facets, add, (zero, zero), unroll=4)


def whole_kernel(
    offsets, owner, counts, sky_own, prolate, table_far, observed_far, uv,
    residual_far, image,
    sky, updates, table, observed, residual, fine, coarse_cos, coarse_sin, modulated, raw,
    turn_cos, turn_sin, lifted, back_cos, back_sin,
    lift_turn_cos, lift_turn_sin, across_cos, across_sin,
    sky_send, sky_recv, update_send, update_recv, local_sem,
):
    slots = observed.shape[0]
    me = lax.axis_index("facet")
    gather = Gather(sky, sky_send, sky_recv)
    back = [
        Gather(updates.at[q], update_send.at[q], update_recv.at[q]) for q in range(slots)
    ]
    load_table = pltpu.make_async_copy(table_far, table, local_sem.at[0])
    load_table.start()
    loads = [
        pltpu.make_async_copy(observed_far.at[q], observed.at[q], local_sem.at[1 + q])
        for q in range(slots)
    ]
    for load in loads:
        load.start()
    barrier = pltpu.get_barrier_semaphore()
    peers = gather.peers()
    for peer in peers:
        pl.semaphore_signal(
            barrier, inc=1, device_id={"facet": peer}, device_id_type=pl.DeviceIdType.MESH
        )
    sky[me] = sky_own[...]
    pl.semaphore_wait(barrier, len(peers))
    gather.start()
    found = slot_scalars(owner, slots)
    phases = (lift_turn_cos, lift_turn_sin, across_cos, across_sin)
    for q in range(slots):
        build_tables(q, uv, fine, coarse_cos, coarse_sin)
        if q == 0:
            gather.relay_first()
        if q == slots - 1:
            gather.relay_second()
    for q in range(slots):
        lift_phases(q, slots, offsets, found, *(ref.at[q] for ref in phases))
    load_table.wait()
    gather.finish()
    stores = []
    for q in range(slots):
        offset = jnp.int32(0)
        live = jnp.int32(0)
        for s, slot in enumerate(found):
            here = slot == me * slots + q
            offset = jnp.where(here, offsets[s], offset)
            live = jnp.where(here, counts[q], live)
        real, imag = forward_slot(
            sky, prolate, offset, table, modulated, raw, turn_cos, turn_sin
        )
        if q > 0:
            back[q - 1].relay_first()
        loads[q].wait()
        result = degrid(
            q, real, imag, live, observed, fine, coarse_cos, coarse_sin, residual,
            back[q - 1].relay_second if q > 0 else lambda: None,
        )
        updates[q, me] = result.astype(jnp.bfloat16)
        back[q].start()
        store = pltpu.make_async_copy(residual.at[q], residual_far.at[q], local_sem.at[1 + slots + q])
        store.start()
        stores.append(store)
    last = back[slots - 1]
    sum_re = sum_im = 0.0
    for q in range(slots):

        def before():
            if q == slots - 1:
                last.relay_second()
            back[q].finish()
            if q == 0 and slots > 1:
                last.relay_first()

        part_re, part_im = lift_slot(
            updates.at[q],
            table,
            before,
            (lifted, back_cos, back_sin) + tuple(ref.at[q] for ref in phases),
        )
        sum_re = sum_re + part_re
        sum_im = sum_im + part_im
    image[0] = sum_re
    image[1] = sum_im
    gather.drain()
    for one in back:
        one.drain()
    for store in stores:
        store.wait()


def last_kernel(scale, residual_in, image_in, prolate, residual, image):
    residual[...] = residual_in[...]
    image[...] = image_in[...] * (prolate[...] * scale)[None]


VMEM = pl.BlockSpec(memory_space=pltpu.VMEM)
SMEM = pl.BlockSpec(memory_space=pltpu.SMEM)
FAR = pl.BlockSpec(memory_space=pl.ANY)


def local(sky_strips, prolate, subgrid_offset, owner, observed, vis_uv, vis_count):
    rows, width = sky_strips.shape[1:]
    facets = lax.axis_size("facet")
    slots, _, _, total = observed.shape
    both = 2 * rows
    table = jnp.asarray(wide_table(width, POINTS, width * facets), jnp.bfloat16)
    f32, bf16 = jnp.float32, jnp.bfloat16
    residual, image = pl.pallas_call(
        whole_kernel,
        out_shape=(
            jax.ShapeDtypeStruct((slots, both, total), bf16),
            jax.ShapeDtypeStruct((2, rows, width), f32),
        ),
        in_specs=[SMEM] * 3 + [VMEM] * 2 + [FAR] * 2 + [VMEM],
        out_specs=(FAR, VMEM),
        scratch_shapes=[
            pltpu.VMEM((facets, both, width), bf16),
            pltpu.VMEM((slots, facets, both, POINTS), bf16),
            pltpu.VMEM(table.shape, bf16),
            pltpu.VMEM(observed.shape, f32),
            pltpu.VMEM((slots, both, total), bf16),
            pltpu.VMEM((slots, 2 * FINE, total), bf16),
            pltpu.VMEM((slots, 8, total), f32),
            pltpu.VMEM((slots, 8, total), f32),
            pltpu.VMEM((facets, both, width), bf16),
            pltpu.VMEM((facets, both, 2 * POINTS), f32),
            pltpu.VMEM((facets, POINTS), f32),
            pltpu.VMEM((facets, POINTS), f32),
            pltpu.VMEM((facets, both, POINTS), bf16),
            pltpu.VMEM((facets, both, width), f32),
            pltpu.VMEM((facets, both, width), f32),
            pltpu.VMEM((slots, facets, POINTS), f32),
            pltpu.VMEM((slots, facets, POINTS), f32),
            pltpu.VMEM((slots, facets, width), f32),
            pltpu.VMEM((slots, facets, width), f32),
            pltpu.SemaphoreType.DMA((3, facets)),
            pltpu.SemaphoreType.DMA((facets,)),
            pltpu.SemaphoreType.DMA((slots, 3, facets)),
            pltpu.SemaphoreType.DMA((slots, facets)),
            pltpu.SemaphoreType.DMA((1 + 2 * slots,)),
        ],
        compiler_params=pltpu.CompilerParams(
            collective_id=0, has_side_effects=True, vmem_limit_bytes=56 * 1024 * 1024
        ),
    )(
        subgrid_offset,
        owner,
        vis_count,
        sky_strips.reshape(both, width),
        prolate[None, :],
        table,
        observed,
        vis_uv,
    )
    residual, image = pl.pallas_call(
        functools.partial(last_kernel, 1.0 / math.sqrt(subgrid_offset.shape[0] * POINTS)),
        out_shape=(
            jax.ShapeDtypeStruct((slots, both, total), bf16),
            jax.ShapeDtypeStruct((2, rows, width), f32),
        ),
        in_specs=[VMEM, VMEM, VMEM],
        out_specs=(VMEM, VMEM),
    )(residual, image, prolate[None, :])
    return residual.reshape(slots, 2, rows, total), image


def solution(mesh):
    in_specs = (
        P(None, "groups", "facet"),
        P(),
        P(),
        P(),
        P(("groups", "facet"), None, None, None),
        P(("groups", "facet"), None),
        P(("groups", "facet")),
    )
    out_specs = (P(("groups", "facet"), None, None, None), P(None, "groups", "facet"))
    return jax.shard_map(local, mesh=mesh, in_specs=in_specs, out_specs=out_specs, check_vma=False)
```
